32 devices in a mesh: groups: 2 (over y), region: 4 (over z), sub: 4 (over x, core).
Axes of the slice: x: 2, y: 2, z: 4, core: 2. Of those that a mesh axis runs over, the one named last changes fastest.
Arguments:
- latents: bfloat16 [32768, 128], P(('groups', 'region', 'sub')), parts along dimension 0, may hold values from -6 to 6
- cotangent: bfloat16 [32768, 128], P(('groups', 'region', 'sub')), parts along dimension 0, may hold values from -6 to 6
- inner_edges: int32 [2, 98304], P(None, ('groups', 'region', 'sub')), parts along dimension 1, may hold values from 0 to 1023
- cut_cells: int32 [24576], P(('groups', 'region', 'sub')), parts along dimension 0, may hold values from 0 to 1023
- pair_count: int32 [384], P(('groups', 'region', 'sub')), parts along dimension 0, may hold values from 0 to 64, as said below
- in_weight: bfloat16 [256, 128], replicated, may hold values from -0.375 to 0.375
- in_bias: float32 [128], replicated, may hold values from -3 to 3
- out_weight: bfloat16 [128, 128], replicated, may hold values from -0.5 to 0.5
- out_bias: float32 [128], replicated, may hold values from -3 to 3
Outputs:
- new_latents: bfloat16 [32768, 128], P(('groups', 'region', 'sub')), parts along dimension 0
- latent_grad: bfloat16 [32768, 128], P(('groups', 'region', 'sub')), parts along dimension 0
- in_weight_step: float32 [512, 128], P('groups'), parts along dimension 0
- in_bias_step: float32 [256], P('groups'), parts along dimension 0
- out_weight_step: float32 [256, 128], P('groups'), parts along dimension 0
- out_bias_step: float32 [256], P('groups'), parts along dimension 0
The draws below stay inside these ranges and needn't reach their ends.
There are 2 independent parts, one for each index of `groups`. The reference program is written for one: setup_inputs(seed, part) draws one part's arguments, and reference() takes and returns one part's arrays. A program takes and returns all parts, laid end to end along the dimension named above; an argument that names none is the same for every part. Nothing has to cross between parts.
Inputs may be any that keep to these rules, and one draw needn't show every extreme that they name: `inner_edges`: local cell numbers within the subdomain that holds the edge. `cut_cells`: slot k of pair list (o, t) of subdomain p, for k below that list's count, is p's cell of the pair's k-th cut edge; the other subdomain of the pair lists the same edges in the same order. Slots at or above the count are padding. `pair_count`: the count of pair list (o, t) of subdomain p counts the cut edges between p and the subdomain at region (region of p + o - 1) modulo the number of regions and sub t; both subdomains of a pair hold the same count, and a subdomain's list with itself has count 0.
All inputs are finite; a program needn't handle non-finite values.
Results may differ from the reference program's by a relative error of at most 0.0055.
Values may be sent and summed in bfloat16 or wider, within the bound.
A program may use at most 64 MiB of HBM per device.

```python
import jax
import jax.numpy as jnp
from jax import lax

C = 128
H = 128
CELLS_DEV = 1024
K = 64
EDGES_DEV = 3072
PARTS_SIZE = 16
PEERS = 12
CELLS = 16384
EDGES = 49152
N_REGION = 4
N_SUB = 4


def draw_pair_count(key, part):
    key = jax.random.fold_in(key, 11)
    subparts = PEERS // 3
    regions = PARTS_SIZE // subparts
    pair_table = jnp.minimum(jax.random.randint(key, (PARTS_SIZE, PARTS_SIZE), K // 4, 2 * K), K)
    part_rank = jnp.arange(PARTS_SIZE, dtype=jnp.int32)
    offsets = jnp.arange(3, dtype=jnp.int32)
    peer_rank = ((part_rank[:, None] // subparts + offsets[None, :] - 1) % regions)[:, :, None] * subparts + jnp.arange(subparts, dtype=jnp.int32)[None, None, :]
    self_rank = jnp.broadcast_to(part_rank[:, None, None], peer_rank.shape)
    lower_rank = jnp.minimum(self_rank, peer_rank)
    upper_rank = jnp.maximum(self_rank, peer_rank)
    tallies = pair_table[lower_rank, upper_rank]
    tallies = jnp.where((lower_rank == 0) & (upper_rank == subparts), K, tallies)
    tallies = jnp.where(self_rank == peer_rank, 0, tallies)
    return tallies.reshape(-1).astype(jnp.int32)


def with_ends(array, rng, smallest, high):
    dims = array.shape
    index_at = [jax.random.randint(jax.random.fold_in(rng, axis), (), 0, dims[axis]) for axis in range(len(dims))]
    array = array.at[tuple(index_at)].set(smallest)
    longest = dims.index(max(dims))
    index_at[longest] = (index_at[longest] + 1) % dims[longest]
    return array.at[tuple(index_at)].set(high)


def level_of(own_key, extent, pieces, smallest, largest):
    gain, own = 1.0, jax.random.fold_in(own_key, 6)
    for axis_at, shards_of in pieces:
        steps = jnp.exp(jax.random.uniform(jax.random.fold_in(own, axis_at), (shards_of,), jnp.float32, smallest / len(pieces), largest / len(pieces)))
        gain = gain * jnp.repeat(steps, extent[axis_at] // shards_of).reshape([-1 if axis == axis_at else 1 for axis in range(len(extent))])
    return gain


def bell_draw(stream_key, extent, deviation, bound, split=(), kind=jnp.bfloat16):
    values = deviation * jax.random.normal(stream_key, extent, jnp.float32)
    if split:
        values = values * level_of(stream_key, extent, split, -0.22, 0.18)
    return jnp.clip(values, -bound, bound).astype(kind)


def setup_inputs(seed: int = 0, part: int = 0) -> dict:
    key_of = jax.random.split(jax.random.key(seed), 10)
    part_keys = jax.random.split(jax.random.fold_in(key_of[9], part), 10)
    latents = bell_draw(part_keys[0], (CELLS, C), 1.0, 6.0, ((0, 16),))
    cotangent = bell_draw(part_keys[1], (CELLS, C), 1.0, 6.0, ((0, 16),))
    inner_edges = with_ends(jax.random.randint(part_keys[2], (2, EDGES), 0, CELLS_DEV), jax.random.fold_in(part_keys[2], 1), 0, CELLS_DEV - 1).astype(jnp.int32)
    cut_cells = with_ends(jax.random.randint(part_keys[3], (PARTS_SIZE * PEERS * K,), 0, CELLS_DEV), jax.random.fold_in(part_keys[3], 1), 0, CELLS_DEV - 1).astype(jnp.int32)
    pair_count = draw_pair_count(jax.random.fold_in(jax.random.fold_in(key_of[9], part), 71), part)
    in_weight = bell_draw(key_of[5], (2 * C, H), (2 * C) ** -0.5, 0.375)
    in_bias = bell_draw(key_of[6], (H,), 0.5, 3.0, (), jnp.float32)
    out_weight = bell_draw(key_of[7], (H, C), H ** -0.5, 0.5)
    out_bias = bell_draw(key_of[8], (C,), 0.5, 3.0, (), jnp.float32)
    return dict(latents=latents, cotangent=cotangent, inner_edges=inner_edges, cut_cells=cut_cells, pair_count=pair_count, in_weight=in_weight, in_bias=in_bias, out_weight=out_weight, out_bias=out_bias)


def flux_forward(inputs, in_weight, in_bias, out_weight, out_bias):
    before = jnp.dot(inputs, in_weight, preferred_element_type=jnp.float32) + in_bias
    hidden = jax.nn.silu(before).astype(jnp.bfloat16)
    flux_rows = (jnp.dot(hidden, out_weight, preferred_element_type=jnp.float32) + out_bias).astype(jnp.bfloat16)
    return (before, hidden, flux_rows)

def flux_backward(before, d_flux, in_weight, out_weight):
    d_hidden = jnp.dot(d_flux, out_weight.T, preferred_element_type=jnp.float32)
    logistic = jax.nn.sigmoid(before)
    d_before = (d_hidden * logistic * (1.0 + before * (1.0 - logistic))).astype(jnp.bfloat16)
    d_inputs = jnp.dot(d_before, in_weight.T, preferred_element_type=jnp.float32).astype(jnp.bfloat16)
    return (d_before, d_inputs)

def weight_terms(inputs, hidden, d_before, d_flux):
    over_rows = (((0,), (0,)), ((), ()))
    return (lax.dot_general(inputs, d_before, over_rows, preferred_element_type=jnp.float32), lax.optimization_barrier(jnp.sum(d_before.astype(jnp.float32), axis=0)), lax.dot_general(hidden, d_flux, over_rows, preferred_element_type=jnp.float32), lax.optimization_barrier(jnp.sum(d_flux.astype(jnp.float32), axis=0)))

def normalized(gradient):
    return gradient / jnp.sqrt(jnp.mean(gradient * gradient) + 1e-06)

def reference(latents, cotangent, inner_edges, cut_cells, pair_count, in_weight, in_bias, out_weight, out_bias):
    part_total = N_REGION * N_SUB
    channels = latents.shape[1]
    edge_part = jnp.arange(EDGES, dtype=jnp.int32) // EDGES_DEV
    inner_head = inner_edges[0] + edge_part * CELLS_DEV
    inner_tail = inner_edges[1] + edge_part * CELLS_DEV
    slot_cells = cut_cells.reshape(part_total, 3, N_SUB, K)
    slot_counts = pair_count.reshape(part_total, 3, N_SUB)
    part_rank = jnp.arange(part_total, dtype=jnp.int32)
    offsets = jnp.arange(3, dtype=jnp.int32)
    peer_rank = ((part_rank[:, None] // N_SUB + offsets[None, :] - 1) % N_REGION)[:, :, None] * N_SUB + jnp.arange(N_SUB, dtype=jnp.int32)[None, None, :]
    mirror_slot = jnp.broadcast_to((2 - offsets)[None, :, None], peer_rank.shape)
    own_sub = jnp.broadcast_to((part_rank % N_SUB)[:, None, None], peer_rank.shape)
    peer_cells = slot_cells[peer_rank, mirror_slot, own_sub]
    slot_index = jnp.arange(K, dtype=jnp.int32)
    owned_live = (slot_index[None, None, None, :] < slot_counts[:, :, :, None]) & (part_rank[:, None, None, None] < peer_rank[:, :, :, None])
    cut_head = (slot_cells + part_rank[:, None, None, None] * CELLS_DEV).reshape(-1)
    cut_tail = (peer_cells + peer_rank[:, :, :, None] * CELLS_DEV).reshape(-1)
    heads = jnp.concatenate([inner_head, cut_head]).astype(jnp.int32)
    tails = jnp.concatenate([inner_tail, cut_tail]).astype(jnp.int32)
    live_rows = jnp.concatenate([jnp.ones((EDGES,), jnp.float32), owned_live.reshape(-1).astype(jnp.float32)])
    edge_total = heads.shape[0]
    block_size = 4096
    padded = -(-edge_total // block_size) * block_size
    heads = jnp.pad(heads, (0, padded - edge_total)).reshape(-1, block_size)
    tails = jnp.pad(tails, (0, padded - edge_total)).reshape(-1, block_size)
    live_rows = jnp.pad(live_rows, (0, padded - edge_total)).reshape(-1, block_size)

    def edge_block(running, block_rows):
        shifted, returned, grad_sums = running
        head_cell, tail_cell, live_mask = block_rows
        inputs = jnp.concatenate([latents[head_cell], latents[tail_cell]], axis=1)
        before, hidden, flux_rows = flux_forward(inputs, in_weight, in_bias, out_weight, out_bias)
        flux_wide = flux_rows.astype(jnp.float32) * live_mask[:, None]
        shifted = shifted.at[head_cell].add(flux_wide).at[tail_cell].add(-flux_wide)
        d_flux = ((cotangent[head_cell].astype(jnp.float32) - cotangent[tail_cell].astype(jnp.float32)) * live_mask[:, None]).astype(jnp.bfloat16)
        d_before, d_inputs = flux_backward(before, d_flux, in_weight, out_weight)
        spread = d_inputs.astype(jnp.float32)
        returned = returned.at[head_cell].add(spread[:, :channels]).at[tail_cell].add(spread[:, channels:])
        grad_sums = jax.tree.map(jnp.add, grad_sums, weight_terms(inputs, hidden, d_before, d_flux))
        return ((shifted, returned, grad_sums), None)
    zero_sums = (jnp.zeros(in_weight.shape, jnp.float32), jnp.zeros(in_bias.shape, jnp.float32), jnp.zeros(out_weight.shape, jnp.float32), jnp.zeros(out_bias.shape, jnp.float32))
    initial = (jnp.zeros(latents.shape, jnp.float32), jnp.zeros(latents.shape, jnp.float32), zero_sums)
    (shifted, returned, grad_sums), unused = lax.scan(edge_block, initial, (heads, tails, live_rows))
    new_latents = (latents.astype(jnp.float32) + shifted).astype(jnp.bfloat16)
    latent_grad = (cotangent.astype(jnp.float32) + returned).astype(jnp.bfloat16)
    return (new_latents, latent_grad, normalized(grad_sums[0]), normalized(grad_sums[1]), normalized(grad_sums[2]), normalized(grad_sums[3]))
```

```python
import functools

import jax
import jax.numpy as jnp
from jax import lax
from jax.experimental import pallas as pl
from jax.experimental.pallas import tpu as pltpu
from jax.sharding import PartitionSpec as P

MESH = pl.DeviceIdType.MESH


def round_up(value, step):
    return -(-value // step) * step


def device_at(rank, subparts):
    return {"region": rank // subparts, "sub": lax.rem(rank, subparts)}


def high_low(value):
    high = value.astype(jnp.bfloat16).astype(jnp.float32)
    return high, value - high


def greet_all(me, total, subparts):
    barrier = pltpu.get_barrier_semaphore()

    def greet(step, unused):
        peer = lax.rem(me + step, total)
        pl.semaphore_signal(barrier, inc=1, device_id=device_at(peer, subparts), device_id_type=MESH)
        return unused

    lax.fori_loop(1, total, greet, 0)
    pl.semaphore_wait(barrier, total - 1)


def exchange(me, total, subparts, source, target, send_sem, recv_sem):
    def copy_of(step):
        peer = lax.rem(me + step, total)
        return pltpu.make_async_remote_copy(
            src_ref=source(peer),
            dst_ref=target(step),
            send_sem=send_sem.at[step],
            recv_sem=recv_sem.at[step],
            device_id=device_at(peer, subparts),
            device_id_type=MESH,
        )

    def begin(step, unused):
        copy_of(step).start()
        return unused

    def finish(step, unused):
        copy_of(step).wait()
        return unused

    return (
        lambda: lax.fori_loop(1, total, begin, 0),
        lambda: lax.fori_loop(1, total, finish, 0),
    )


def sum_kernel(
    regions, subparts, chunk,
    in_weight, in_bias, out_weight, out_bias,
    in_weight_out, in_bias_out, out_weight_out, out_bias_out,
    terms, sent, landed, gathered, send_a, recv_a, send_b, recv_b,
):
    total = regions * subparts
    me = lax.axis_index("region") * subparts + lax.axis_index("sub")
    slot_rows = sent.shape[1]
    wide = in_weight.shape[0]
    narrow = out_weight.shape[0]
    greet_all(me, total, subparts)
    terms[0:wide] = in_weight[...]
    terms[wide : wide + narrow] = out_weight[...]
    terms[wide + narrow :] = jnp.zeros((terms.shape[0] - wide - narrow, terms.shape[1]), jnp.float32)
    bias_rows = jnp.concatenate(
        [*high_low(in_bias[...]), *high_low(out_bias[...]),
         jnp.zeros((slot_rows - chunk - 4, terms.shape[1]), jnp.float32)], axis=0
    )

    def fill(rank, unused):
        part = terms[pl.ds(pl.multiple_of(rank * chunk, 8), chunk)]
        sent[rank] = jnp.concatenate([part, bias_rows], axis=0).astype(jnp.bfloat16)
        return unused

    lax.fori_loop(0, total, fill, 0)
    begin, finish = exchange(
        me, total, subparts, lambda peer: sent.at[peer], lambda step: landed.at[step], send_a, recv_a
    )
    begin()
    landed[0] = sent[me]
    finish()
    owned = jnp.sum(landed[...].astype(jnp.float32), axis=0)
    gathered[me] = owned.astype(jnp.bfloat16)
    begin, finish = exchange(
        me, total, subparts, lambda peer: gathered.at[me], lambda step: gathered.at[me], send_b, recv_b
    )
    begin()
    in_bias_out[...] = normalized(owned[chunk : chunk + 1] + owned[chunk + 1 : chunk + 2])
    out_bias_out[...] = normalized(owned[chunk + 2 : chunk + 3] + owned[chunk + 3 : chunk + 4])
    finish()
    everything = gathered[...].astype(jnp.float32)[:, :chunk].reshape(total * chunk, -1)
    in_weight_out[...] = normalized(everything[:wide])
    out_weight_out[...] = normalized(everything[wide : wide + narrow])


def summed_steps(in_weight, in_bias, out_weight, out_bias):
    regions = lax.axis_size("region")
    subparts = lax.axis_size("sub")
    total = regions * subparts
    wide, lanes = in_weight.shape
    narrow = out_weight.shape[0]
    chunk = round_up(-(-(wide + narrow) // total), 8)
    slot_rows = round_up(chunk + 4, 16)
    vmem = pl.BlockSpec(memory_space=pltpu.VMEM)
    f32 = jnp.float32
    a, b, c, d = pl.pallas_call(
        functools.partial(sum_kernel, regions, subparts, chunk),
        out_shape=[
            jax.ShapeDtypeStruct((wide, lanes), f32),
            jax.ShapeDtypeStruct((1, lanes), f32),
            jax.ShapeDtypeStruct((narrow, out_weight.shape[1]), f32),
            jax.ShapeDtypeStruct((1, out_weight.shape[1]), f32),
        ],
        in_specs=[vmem] * 4,
        out_specs=[vmem] * 4,
        scratch_shapes=[
            pltpu.VMEM((max(total * chunk, wide + narrow + 8), lanes), f32),
            pltpu.VMEM((total, slot_rows, lanes), jnp.bfloat16),
            pltpu.VMEM((total, slot_rows, lanes), jnp.bfloat16),
            pltpu.VMEM((total, slot_rows, lanes), jnp.bfloat16),
            pltpu.SemaphoreType.DMA((total,)),
            pltpu.SemaphoreType.DMA((total,)),
            pltpu.SemaphoreType.DMA((total,)),
            pltpu.SemaphoreType.DMA((total,)),
        ],
        compiler_params=pltpu.CompilerParams(collective_id=0, has_side_effects=True),
    )(in_weight, in_bias[None], out_weight, out_bias[None])
    return a, b[0], c, d[0]


def from_behind(block, axis, distance):
    devices = range(lax.axis_size(axis))
    route = [((i - distance) % len(devices), i) for i in devices]
    return lax.ppermute(block, axis, route)


def flux_forward(inputs, in_weight, in_bias, out_weight, out_bias):
    before = jnp.dot(inputs, in_weight, preferred_element_type=jnp.float32) + in_bias
    hidden = jax.nn.silu(before).astype(jnp.bfloat16)
    flux_rows = (jnp.dot(hidden, out_weight, preferred_element_type=jnp.float32) + out_bias).astype(
        jnp.bfloat16
    )
    return (before, hidden, flux_rows)


def flux_backward(before, d_flux, in_weight, out_weight):
    d_hidden = jnp.dot(d_flux, out_weight.T, preferred_element_type=jnp.float32)
    logistic = jax.nn.sigmoid(before)
    d_before = (d_hidden * logistic * (1.0 + before * (1.0 - logistic))).astype(jnp.bfloat16)
    d_inputs = jnp.dot(d_before, in_weight.T, preferred_element_type=jnp.float32).astype(
        jnp.bfloat16
    )
    return (d_before, d_inputs)


def weight_terms(inputs, hidden, d_before, d_flux):
    over_rows = (((0,), (0,)), ((), ()))
    return (
        lax.dot_general(inputs, d_before, over_rows, preferred_element_type=jnp.float32),
        jnp.sum(d_before.astype(jnp.float32), axis=0),
        lax.dot_general(hidden, d_flux, over_rows, preferred_element_type=jnp.float32),
        jnp.sum(d_flux.astype(jnp.float32), axis=0),
    )


def normalized(gradient):
    return gradient / jnp.sqrt(jnp.mean(gradient * gradient) + 1e-06)


def cell_table(cells, cell_count):
    return (cells[:, None] == jnp.arange(cell_count, dtype=jnp.int32)[None, :]).astype(jnp.bfloat16)


def pick_rows(table, data):
    return jnp.dot(table, data, preferred_element_type=jnp.float32).astype(jnp.bfloat16)


def spread_rows(table, pieces):
    return lax.dot_general(
        table, pieces, (((0,), (0,)), ((), ())), preferred_element_type=jnp.float32
    )


def route(pieces):
    crossed = lax.all_to_all(pieces, "sub", split_axis=1, concat_axis=1, tiled=True)
    landed = [crossed[1], crossed[1], crossed[1]]
    for hop_by, from_slot, to_slot in ((1, 2, 0), (-1, 0, 2)):
        landed[to_slot] = from_behind(crossed[from_slot], "region", hop_by)
    return jnp.stack(landed, axis=0)


def local(
    latents, cotangent, inner_edges, cut_cells, pair_count, in_weight, in_bias, out_weight, out_bias
):
    channels = latents.shape[1]
    cell_count = latents.shape[0]
    edge_total = inner_edges.shape[1]
    block_size = 1024
    both_fields = jnp.concatenate([latents, cotangent], axis=1)

    def edge_block(running, block_rows):
        accum, grad_sums = running
        head_table = cell_table(block_rows[0], cell_count)
        tail_table = cell_table(block_rows[1], cell_count)
        head_rows = pick_rows(head_table, both_fields)
        tail_rows = pick_rows(tail_table, both_fields)
        inputs = jnp.concatenate([head_rows[:, :channels], tail_rows[:, :channels]], axis=1)
        before, hidden, flux_rows = flux_forward(inputs, in_weight, in_bias, out_weight, out_bias)
        d_flux = (
            head_rows[:, channels:].astype(jnp.float32)
            - tail_rows[:, channels:].astype(jnp.float32)
        ).astype(jnp.bfloat16)
        d_before, d_inputs = flux_backward(before, d_flux, in_weight, out_weight)
        head_pieces = jnp.concatenate([flux_rows, d_inputs[:, :channels]], axis=1)
        tail_pieces = jnp.concatenate([-flux_rows, d_inputs[:, channels:]], axis=1)
        accum = accum + spread_rows(head_table, head_pieces) + spread_rows(tail_table, tail_pieces)
        grad_sums = jax.tree.map(jnp.add, grad_sums, weight_terms(inputs, hidden, d_before, d_flux))
        return ((accum, grad_sums), None)

    blocks = jnp.transpose(inner_edges.reshape(2, edge_total // block_size, block_size), (1, 0, 2))
    zero_sums = (
        jnp.zeros(in_weight.shape, jnp.float32),
        jnp.zeros(in_bias.shape, jnp.float32),
        jnp.zeros(out_weight.shape, jnp.float32),
        jnp.zeros(out_bias.shape, jnp.float32),
    )
    initial = (jnp.zeros((cell_count, 2 * channels), jnp.float32), zero_sums)
    (accum, grad_sums), unused = lax.scan(edge_block, initial, blocks)
    regions = lax.axis_size("region")
    subparts = lax.axis_size("sub")
    region = lax.axis_index("region")
    subpart = lax.axis_index("sub")
    slot_cells = cut_cells.reshape(3, subparts, -1)
    slot_total = slot_cells.shape[2]
    offsets = jnp.arange(3, dtype=jnp.int32)
    peer_rank = ((region + offsets - 1) % regions)[:, None] * subparts + jnp.arange(
        subparts, dtype=jnp.int32
    )[None, :]
    own_rank = region * subparts + subpart
    leading = own_rank < peer_rank
    live_slots = (
        jnp.arange(slot_total, dtype=jnp.int32)[None, None, :]
        < pair_count.reshape(3, subparts)[:, :, None]
    )
    slot_table = cell_table(cut_cells, cell_count)
    own_rows = pick_rows(slot_table, both_fields).reshape(3, subparts, slot_total, 2 * channels)
    own_latents = own_rows[..., :channels]
    own_cotangent = own_rows[..., channels:]
    incoming = route(own_rows)
    peer_latents = incoming[..., :channels]
    peer_cotangent = incoming[..., channels:]
    lead_rows = leading[:, :, None, None]
    live_wide = live_slots[..., None].astype(jnp.bfloat16)
    head_latents = jnp.where(lead_rows, own_latents, peer_latents)
    tail_latents = jnp.where(lead_rows, peer_latents, own_latents)
    head_cotangent = jnp.where(lead_rows, own_cotangent, peer_cotangent)
    tail_cotangent = jnp.where(lead_rows, peer_cotangent, own_cotangent)
    inputs = jnp.concatenate([head_latents, tail_latents], axis=3).reshape(-1, 2 * channels)
    before, hidden, flux_rows = flux_forward(inputs, in_weight, in_bias, out_weight, out_bias)
    flux_live = flux_rows.reshape(3, subparts, slot_total, channels) * live_wide
    cut_shift = jnp.where(lead_rows, flux_live, -flux_live)
    d_flux = (
        (
            (head_cotangent.astype(jnp.float32) - tail_cotangent.astype(jnp.float32))
            * live_wide.astype(jnp.float32)
        )
        .astype(jnp.bfloat16)
        .reshape(-1, channels)
    )
    d_before, d_inputs = flux_backward(before, d_flux, in_weight, out_weight)
    spread = d_inputs.reshape(3, subparts, slot_total, 2 * channels)
    cut_return = jnp.where(lead_rows, spread[..., :channels], spread[..., channels:])
    cut_pieces = jnp.concatenate([cut_shift, cut_return], axis=3).reshape(-1, 2 * channels)
    accum = accum + spread_rows(slot_table, cut_pieces)
    owned_rows = (live_slots & leading[:, :, None]).reshape(-1, 1).astype(jnp.bfloat16)
    cut_terms = weight_terms(inputs, hidden, d_before * owned_rows, d_flux * owned_rows)
    grad_sums = jax.tree.map(jnp.add, grad_sums, cut_terms)
    in_weight_sum, in_bias_sum, out_weight_sum, out_bias_sum = grad_sums
    steps = summed_steps(in_weight_sum, in_bias_sum, out_weight_sum, out_bias_sum)
    new_latents = (latents.astype(jnp.float32) + accum[:, :channels]).astype(jnp.bfloat16)
    latent_grad = (cotangent.astype(jnp.float32) + accum[:, channels:]).astype(jnp.bfloat16)
    return (
        new_latents,
        latent_grad,
        *steps,
    )


def solution(mesh):
    placed = (
        P(("groups", "region", "sub"), None),
        P(("groups", "region", "sub"), None),
        P(None, ("groups", "region", "sub")),
        P(("groups", "region", "sub")),
        P(("groups", "region", "sub")),
        P(),
        P(),
        P(),
        P(),
    )
    return jax.shard_map(
        local,
        mesh=mesh,
        in_specs=placed,
        out_specs=(
            P(("groups", "region", "sub"), None),
            P(("groups", "region", "sub"), None),
            P("groups", None),
            P("groups"),
            P("groups", None),
            P("groups"),
        ),
        check_vma=False,
    )
```

```python
import functools

import jax
import jax.numpy as jnp
from jax import lax
from jax.experimental import pallas as pl
from jax.experimental.pallas import tpu as pltpu
from jax.sharding import PartitionSpec as P

MESH = pl.DeviceIdType.MESH


def round_up(value, step):
    return -(-value // step) * step


def device_at(rank, subparts):
    return {"region": rank // subparts, "sub": lax.rem(rank, subparts)}


def high_low(value):
    high = value.astype(jnp.bfloat16).astype(jnp.float32)
    return high, value - high


def exchange(me, total, subparts, source, target, send_sem, recv_sem):
    def copy_of(step):
        peer = lax.rem(me + step, total)
        return pltpu.make_async_remote_copy(
            src_ref=source(peer),
            dst_ref=target(step),
            send_sem=send_sem.at[step],
            recv_sem=recv_sem.at[step],
            device_id=device_at(peer, subparts),
            device_id_type=MESH,
        )

    def begin(step, unused):
        copy_of(step).start()
        return unused

    def finish(step, unused):
        copy_of(step).wait()
        return unused

    return (
        lambda: lax.fori_loop(1, total, begin, 0),
        lambda: lax.fori_loop(1, total, finish, 0),
    )


def normalized(gradient):
    return gradient / jnp.sqrt(jnp.mean(gradient * gradient) + 1e-06)


def dot(left, right, left_axis=1, right_axis=0):
    return lax.dot_general(
        left, right, (((left_axis,), (right_axis,)), ((), ())), preferred_element_type=jnp.float32
    )


def one_hot(match):
    return jnp.where(match, 1.0, 0.0).astype(jnp.bfloat16)


def edge_by_cell(cell_row, cell_count):
    rows = cell_row.shape[1]
    spread = jnp.transpose(jnp.broadcast_to(cell_row, (128, rows)))
    lane = lax.broadcasted_iota(jnp.int32, (rows, 128), 1)
    return jnp.concatenate(
        [one_hot(spread == lane + start) for start in range(0, cell_count, 128)], axis=1
    )


def cell_by_edge(cell_row, cell_count):
    cell = lax.broadcasted_iota(jnp.int32, (cell_count, cell_row.shape[1]), 0)
    return one_hot(cell == cell_row)


def edge_network(head_rows, tail_rows, live, in_weight, in_bias, out_weight, out_bias):
    channels = out_weight.shape[1]
    inputs = jnp.concatenate([head_rows[:, :channels], tail_rows[:, :channels]], axis=1)
    before = dot(inputs, in_weight) + in_bias
    logistic = 1.0 / (1.0 + jnp.exp(-before))
    hidden = (before * logistic).astype(jnp.bfloat16)
    flux = (dot(hidden, out_weight) + out_bias).astype(jnp.bfloat16)
    d_flux = head_rows[:, channels:].astype(jnp.float32) - tail_rows[:, channels:].astype(jnp.float32)
    if live is not None:
        d_flux = d_flux * live
    d_flux = d_flux.astype(jnp.bfloat16)
    d_hidden = dot(d_flux, out_weight, 1, 1)
    d_before = (d_hidden * logistic * (1.0 + before * (1.0 - logistic))).astype(jnp.bfloat16)
    d_inputs = dot(d_before, in_weight, 1, 1).astype(jnp.bfloat16)
    return inputs, hidden, flux, d_flux, d_before, d_inputs


def layer_kernel(
    regions, subparts, chunk, block,
    latents, cotangent, edges, cut_cells, pair_count, in_weight, in_bias, out_weight, out_bias,
    new_latents, latent_grad, in_weight_out, in_bias_out, out_weight_out, out_bias_out,
    both, own, incoming, heads, tails, live_rows, lead_rows, pieces, cut_pieces, accum,
    terms, bias_terms, sent, landed, gathered,
    cut_send, cut_recv, send_a, recv_a, send_b, recv_b,
):
    total = regions * subparts
    region = lax.axis_index("region")
    subpart = lax.axis_index("sub")
    me = region * subparts + subpart
    cell_count, channels = latents.shape
    wide = in_weight.shape[0]
    narrow = out_weight.shape[0]
    slot_rows = sent.shape[1]
    lists, slots = own.shape[0], own.shape[1]
    blocks = edges.shape[1] // block
    f32 = jnp.float32

    barrier = pltpu.get_barrier_semaphore()

    def greet(step, unused):
        peer = lax.rem(me + step, total)
        pl.semaphore_signal(barrier, inc=1, device_id=device_at(peer, subparts), device_id_type=MESH)
        return unused

    lax.fori_loop(1, total, greet, 0)

    both[:, :channels] = latents[...]
    both[:, channels:] = cotangent[...]
    terms[...] = jnp.zeros(terms.shape, f32)
    bias_terms[...] = jnp.zeros(bias_terms.shape, f32)
    group = subparts * slots

    def pick_cut(offset, unused):
        at = pl.multiple_of(offset * group, 128)
        table = edge_by_cell(cut_cells[:, pl.ds(at, group)], cell_count)
        rows = dot(table, both[...]).astype(jnp.bfloat16)
        own[pl.ds(offset * subparts, subparts)] = rows.reshape(subparts, slots, 2 * channels)
        return unused

    lax.fori_loop(0, 3, pick_cut, 0)
    incoming[subparts + subpart] = jnp.zeros((slots, 2 * channels), jnp.bfloat16)
    pl.semaphore_wait(barrier, total - 1)

    def cut_copy(index):
        offset = index // subparts
        other = lax.rem(index, subparts)
        there = (2 - offset) * subparts + subpart
        return pltpu.make_async_remote_copy(
            src_ref=own.at[index],
            dst_ref=incoming.at[there],
            send_sem=cut_send.at[index],
            recv_sem=cut_recv.at[there],
            device_id={"region": lax.rem(region + offset + regions - 1, regions), "sub": other},
            device_id_type=MESH,
        )

    def landed_copy(index):
        return pltpu.make_async_remote_copy(
            src_ref=own.at[index],
            dst_ref=incoming.at[index],
            send_sem=cut_send.at[index],
            recv_sem=cut_recv.at[index],
            device_id={
                "region": lax.rem(region + index // subparts + regions - 1, regions),
                "sub": lax.rem(index, subparts),
            },
            device_id_type=MESH,
        )

    def send_cut(index, unused):
        @pl.when(index != subparts + subpart)
        def begin():
            cut_copy(index).start()

        return unused

    lax.fori_loop(0, lists, send_cut, 0)

    def add_terms(inputs, hidden, d_before, d_flux):
        terms[0:wide] += dot(inputs, d_before, 0, 0)
        terms[wide : wide + narrow] += dot(hidden, d_flux, 0, 0)
        bias_terms[0:1] += jnp.sum(d_before.astype(f32), axis=0, keepdims=True)
        bias_terms[1:2] += jnp.sum(d_flux.astype(f32), axis=0, keepdims=True)

    def interior(index, unused):
        at = pl.multiple_of(index * block, 128)
        head_rows = dot(edge_by_cell(edges[0:1, pl.ds(at, block)], cell_count), both[...])
        tail_rows = dot(edge_by_cell(edges[1:2, pl.ds(at, block)], cell_count), both[...])
        inputs, hidden, flux, d_flux, d_before, d_inputs = edge_network(
            head_rows.astype(jnp.bfloat16), tail_rows.astype(jnp.bfloat16), None,
            in_weight[...], in_bias[...], out_weight[...], out_bias[...],
        )
        pieces[index, 0:block, :channels] = flux
        pieces[index, 0:block, channels:] = d_inputs[:, :channels]
        pieces[index, block:, :channels] = -flux
        pieces[index, block:, channels:] = d_inputs[:, channels:]
        add_terms(inputs, hidden, d_before, d_flux)
        return unused

    lax.fori_loop(0, blocks, interior, 0)

    def arrange(index, unused):
        @pl.when(index != subparts + subpart)
        def finish():
            landed_copy(index).wait_recv()

        offset = index // subparts
        peer = lax.rem(region + offset + regions - 1, regions) * subparts + lax.rem(index, subparts)
        lead = jnp.where(me < peer, 1.0, 0.0)
        at = pl.multiple_of(index * slots, 16)
        mask = jnp.full((slots, 2 * channels), lead, f32) > 0.5
        mine, other = own[index].astype(f32), incoming[index].astype(f32)
        heads[pl.ds(at, slots)] = jnp.where(mask, mine, other).astype(jnp.bfloat16)
        tails[pl.ds(at, slots)] = jnp.where(mask, other, mine).astype(jnp.bfloat16)
        slot = lax.broadcasted_iota(jnp.int32, (slots, channels), 0)
        live_rows[pl.ds(at, slots)] = jnp.where(slot < pair_count[index], 1.0, 0.0)
        lead_rows[pl.ds(at, slots)] = jnp.full((slots, channels), lead, f32)
        return unused

    lax.fori_loop(0, lists, arrange, 0)

    def cut(offset, unused):
        at = pl.multiple_of(offset * group, 128)
        rows = pl.ds(at, group)
        live, lead = live_rows[rows], lead_rows[rows]
        inputs, hidden, flux, d_flux, d_before, d_inputs = edge_network(
            heads[rows], tails[rows], live,
            in_weight[...], in_bias[...], out_weight[...], out_bias[...],
        )
        owned = live * lead
        sign = live * (2.0 * lead - 1.0)
        cut_pieces[rows, :channels] = (flux.astype(f32) * sign).astype(jnp.bfloat16)
        spread = d_inputs.astype(f32)
        cut_pieces[rows, channels:] = jnp.where(
            lead > 0.5, spread[:, :channels], spread[:, channels:]
        ).astype(jnp.bfloat16)
        add_terms(
            inputs, hidden,
            (d_before.astype(f32) * owned).astype(jnp.bfloat16),
            (d_flux.astype(f32) * owned).astype(jnp.bfloat16),
        )
        return unused

    lax.fori_loop(0, 3, cut, 0)

    bias_rows = jnp.concatenate(
        [*high_low(bias_terms[0:1]), *high_low(bias_terms[1:2]),
         jnp.zeros((slot_rows - chunk - 4, channels), f32)], axis=0
    )

    def fill(rank, unused):
        part = terms[pl.ds(pl.multiple_of(rank * chunk, 8), chunk)]
        sent[rank] = jnp.concatenate([part, bias_rows], axis=0).astype(jnp.bfloat16)
        return unused

    lax.fori_loop(0, total, fill, 0)
    begin_a, finish_a = exchange(
        me, total, subparts, lambda peer: sent.at[peer], lambda step: landed.at[step], send_a, recv_a
    )
    begin_a()
    landed[0] = sent[me]

    def spread_block(index, unused):
        at = pl.multiple_of(index * block, 128)
        head_table = cell_by_edge(edges[0:1, pl.ds(at, block)], cell_count)
        tail_table = cell_by_edge(edges[1:2, pl.ds(at, block)], cell_count)
        accum[...] += dot(head_table, pieces[index, 0:block]) + dot(tail_table, pieces[index, block:])
        return unused

    accum[...] = dot(cell_by_edge(cut_cells[...], cell_count), cut_pieces[...])
    first = blocks // 2
    lax.fori_loop(0, first, spread_block, 0)
    finish_a()
    owned_sum = jnp.sum(landed[...].astype(f32), axis=0)
    gathered[me] = owned_sum.astype(jnp.bfloat16)
    begin_b, finish_b = exchange(
        me, total, subparts, lambda peer: gathered.at[me], lambda step: gathered.at[me], send_b, recv_b
    )
    begin_b()
    lax.fori_loop(first, blocks, spread_block, 0)
    in_bias_out[...] = normalized(owned_sum[chunk : chunk + 1] + owned_sum[chunk + 1 : chunk + 2])
    out_bias_out[...] = normalized(owned_sum[chunk + 2 : chunk + 3] + owned_sum[chunk + 3 : chunk + 4])
    new_latents[...] = (latents[...].astype(f32) + accum[:, :channels]).astype(jnp.bfloat16)
    latent_grad[...] = (cotangent[...].astype(f32) + accum[:, channels:]).astype(jnp.bfloat16)

    def sent_cut(index, unused):
        @pl.when(index != subparts + subpart)
        def finish():
            landed_copy(index).wait_send()

        return unused

    lax.fori_loop(0, lists, sent_cut, 0)
    finish_b()
    everything = gathered[...].astype(f32)[:, :chunk].reshape(total * chunk, channels)
    in_weight_out[...] = normalized(everything[:wide])
    out_weight_out[...] = normalized(everything[wide : wide + narrow])


def local(
    latents, cotangent, inner_edges, cut_cells, pair_count, in_weight, in_bias, out_weight, out_bias
):
    regions = lax.axis_size("region")
    subparts = lax.axis_size("sub")
    total = regions * subparts
    cell_count, channels = latents.shape
    edge_total = inner_edges.shape[1]
    wide, hidden = in_weight.shape
    narrow = out_weight.shape[0]
    lists = pair_count.shape[0]
    slots = cut_cells.shape[0] // lists
    cut_total = lists * slots
    block = 1024
    blocks = edge_total // block
    chunk = round_up(-(-(wide + narrow) // total), 8)
    slot_rows = round_up(chunk + 4, 16)
    vmem = pl.BlockSpec(memory_space=pltpu.VMEM)
    smem = pl.BlockSpec(memory_space=pltpu.SMEM)
    f32, bf16 = jnp.float32, jnp.bfloat16
    dma = pltpu.SemaphoreType.DMA
    a, b, c, d, e, f = pl.pallas_call(
        functools.partial(layer_kernel, regions, subparts, chunk, block),
        out_shape=[
            jax.ShapeDtypeStruct((cell_count, channels), bf16),
            jax.ShapeDtypeStruct((cell_count, channels), bf16),
            jax.ShapeDtypeStruct((wide, hidden), f32),
            jax.ShapeDtypeStruct((1, hidden), f32),
            jax.ShapeDtypeStruct((narrow, channels), f32),
            jax.ShapeDtypeStruct((1, channels), f32),
        ],
        in_specs=[vmem] * 4 + [smem] + [vmem] * 4,
        out_specs=[vmem] * 6,
        scratch_shapes=[
            pltpu.VMEM((cell_count, 2 * channels), bf16),
            pltpu.VMEM((lists, slots, 2 * channels), bf16),
            pltpu.VMEM((lists, slots, 2 * channels), bf16),
            pltpu.VMEM((cut_total, 2 * channels), bf16),
            pltpu.VMEM((cut_total, 2 * channels), bf16),
            pltpu.VMEM((cut_total, channels), f32),
            pltpu.VMEM((cut_total, channels), f32),
            pltpu.VMEM((blocks, 2 * block, 2 * channels), bf16),
            pltpu.VMEM((cut_total, 2 * channels), bf16),
            pltpu.VMEM((cell_count, 2 * channels), f32),
            pltpu.VMEM((max(total * chunk, wide + narrow), channels), f32),
            pltpu.VMEM((8, channels), f32),
            pltpu.VMEM((total, slot_rows, channels), bf16),
            pltpu.VMEM((total, slot_rows, channels), bf16),
            pltpu.VMEM((total, slot_rows, channels), bf16),
            dma((lists,)),
            dma((lists,)),
            dma((total,)),
            dma((total,)),
            dma((total,)),
            dma((total,)),
        ],
        compiler_params=pltpu.CompilerParams(
            collective_id=0, has_side_effects=True, vmem_limit_bytes=48 * 1024 * 1024
        ),
    )(
        latents, cotangent, inner_edges, cut_cells[None], pair_count,
        in_weight, in_bias[None], out_weight, out_bias[None],
    )
    return a, b, c, d[0], e, f[0]


def solution(mesh):
    placed = (
        P(("groups", "region", "sub"), None),
        P(("groups", "region", "sub"), None),
        P(None, ("groups", "region", "sub")),
        P(("groups", "region", "sub")),
        P(("groups", "region", "sub")),
        P(),
        P(),
        P(),
        P(),
    )
    return jax.shard_map(
        local,
        mesh=mesh,
        in_specs=placed,
        out_specs=(
            P(("groups", "region", "sub"), None),
            P(("groups", "region", "sub"), None),
            P("groups", None),
            P("groups"),
            P("groups", None),
            P("groups"),
        ),
        check_vma=False,
    )
```

```python
import functools

import jax
import jax.numpy as jnp
from jax import lax
from jax.experimental import pallas as pl
from jax.experimental.pallas import tpu as pltpu
from jax.sharding import PartitionSpec as P

MESH = pl.DeviceIdType.MESH


def round_up(value, step):
    return -(-value // step) * step


def device_at(rank, subparts):
    return {"region": rank // subparts, "sub": lax.rem(rank, subparts)}


def high_low(value):
    high = value.astype(jnp.bfloat16).astype(jnp.float32)
    return high, value - high


def exchange(me, total, subparts, source, target, send_sem, recv_sem):
    def copy_of(step):
        peer = lax.rem(me + step, total)
        return pltpu.make_async_remote_copy(
            src_ref=source(peer),
            dst_ref=target(step),
            send_sem=send_sem.at[step],
            recv_sem=recv_sem.at[step],
            device_id=device_at(peer, subparts),
            device_id_type=MESH,
        )

    def begin(step, unused):
        copy_of(step).start()
        return unused

    def finish(step, unused):
        copy_of(step).wait()
        return unused

    return (
        lambda: lax.fori_loop(1, total, begin, 0),
        lambda: lax.fori_loop(1, total, finish, 0),
    )


def normalized(gradient):
    return gradient / jnp.sqrt(jnp.mean(gradient * gradient) + 1e-06)


def dot(left, right, left_axis=1, right_axis=0):
    return lax.dot_general(
        left, right, (((left_axis,), (right_axis,)), ((), ())), preferred_element_type=jnp.float32
    )


def edge_by_cell(cell_row, cell_count):
    rows = cell_row.shape[1]
    spread = jnp.transpose(jnp.broadcast_to(cell_row, (128, rows)))
    lane = lax.broadcasted_iota(jnp.int32, (rows, 128), 1)
    low = jnp.where(spread & 127 == lane, 1.0, 0.0).astype(jnp.bfloat16)
    high = (lax.shift_right_logical(spread, 7)).astype(jnp.float32).astype(jnp.bfloat16)
    zero = jnp.zeros((rows, 128), jnp.bfloat16)
    return jnp.concatenate(
        [jnp.where(high == jnp.bfloat16(part), low, zero) for part in range(cell_count // 128)], axis=1
    )


def cell_by_edge(cell_row, cell_count):
    rows = cell_row.shape[1]
    spread = jnp.broadcast_to(cell_row, (16, rows))
    cell = lax.broadcasted_iota(jnp.int32, (16, rows), 0)
    low = jnp.where(spread & 15 == cell, 1.0, 0.0).astype(jnp.bfloat16)
    high = (lax.shift_right_logical(spread, 4)).astype(jnp.float32).astype(jnp.bfloat16)
    zero = jnp.zeros((16, rows), jnp.bfloat16)
    return jnp.concatenate(
        [jnp.where(high == jnp.bfloat16(part), low, zero) for part in range(cell_count // 16)], axis=0
    )


def edge_network(head_rows, tail_rows, live, in_weight, in_bias, out_weight, out_bias):
    channels = out_weight.shape[1]
    inputs = jnp.concatenate([head_rows[:, :channels], tail_rows[:, :channels]], axis=1)
    before = dot(inputs, in_weight) + in_bias
    logistic = 1.0 / (1.0 + jnp.exp(-before))
    hidden = (before * logistic).astype(jnp.bfloat16)
    flux = (dot(hidden, out_weight) + out_bias).astype(jnp.bfloat16)
    d_flux = head_rows[:, channels:].astype(jnp.float32) - tail_rows[:, channels:].astype(jnp.float32)
    if live is not None:
        d_flux = d_flux * live
    d_flux = d_flux.astype(jnp.bfloat16)
    d_hidden = dot(d_flux, out_weight, 1, 1)
    d_before = (d_hidden * logistic * (1.0 + before * (1.0 - logistic))).astype(jnp.bfloat16)
    d_inputs = dot(d_before, in_weight, 1, 1).astype(jnp.bfloat16)
    return inputs, hidden, flux, d_flux, d_before, d_inputs


def layer_kernel(
    regions, subparts, chunk, block,
    latents_from, cotangent_from, edges_from, cut_flat, pair_count, in_weight_from, in_bias, out_weight_from, out_bias,
    new_latents, latent_grad, in_weight_out, in_bias_out, out_weight_out, out_bias_out,
    latents, cotangent, edges, cut_cells, in_weight, out_weight, arrived,
    both, own, incoming, heads, tails, live_rows, lead_rows, pieces, cut_pieces, accum,
    terms, bias_terms, sent, landed, gathered,
    cut_send, cut_recv, send_a, recv_a, send_b, recv_b,
):
    total = regions * subparts
    region = lax.axis_index("region")
    subpart = lax.axis_index("sub")
    me = region * subparts + subpart
    cell_count, channels = latents.shape
    wide = in_weight.shape[0]
    narrow = out_weight.shape[0]
    slot_rows = sent.shape[1]
    lists, slots = own.shape[0], own.shape[1]
    blocks = edges.shape[1] // block
    f32 = jnp.float32

    fetches = [
        pltpu.make_async_copy(source, target, arrived.at[place])
        for place, (source, target) in enumerate(
            (
                (latents_from, latents),
                (cotangent_from, cotangent),
                (edges_from, edges),
                (in_weight_from, in_weight),
                (out_weight_from, out_weight),
            )
        )
    ]
    for fetch in fetches:
        fetch.start()
    barrier = pltpu.get_barrier_semaphore()

    def greet(step, unused):
        peer = lax.rem(me + step, total)
        pl.semaphore_signal(barrier, inc=1, device_id=device_at(peer, subparts), device_id_type=MESH)
        return unused

    lax.fori_loop(1, total, greet, 0)

    cut_cells[...] = cut_flat[...].reshape(1, -1)
    for fetch in fetches:
        fetch.wait()
    both[:, :channels] = latents[...]
    both[:, channels:] = cotangent[...]
    terms[...] = jnp.zeros(terms.shape, f32)
    bias_terms[...] = jnp.zeros(bias_terms.shape, f32)
    group = subparts * slots

    def pick_cut(offset, unused):
        at = pl.multiple_of(offset * group, 128)
        table = edge_by_cell(cut_cells[:, pl.ds(at, group)], cell_count)
        rows = dot(table, both[...]).astype(jnp.bfloat16)
        own[pl.ds(offset * subparts, subparts)] = rows.reshape(subparts, slots, 2 * channels)
        return unused

    lax.fori_loop(0, 3, pick_cut, 0)
    incoming[subparts + subpart] = jnp.zeros((slots, 2 * channels), jnp.bfloat16)
    pl.semaphore_wait(barrier, total - 1)

    def cut_copy(index):
        offset = index // subparts
        other = lax.rem(index, subparts)
        there = (2 - offset) * subparts + subpart
        return pltpu.make_async_remote_copy(
            src_ref=own.at[index],
            dst_ref=incoming.at[there],
            send_sem=cut_send.at[index],
            recv_sem=cut_recv.at[there],
            device_id={"region": lax.rem(region + offset + regions - 1, regions), "sub": other},
            device_id_type=MESH,
        )

    def landed_copy(index):
        return pltpu.make_async_remote_copy(
            src_ref=own.at[index],
            dst_ref=incoming.at[index],
            send_sem=cut_send.at[index],
            recv_sem=cut_recv.at[index],
            device_id={
                "region": lax.rem(region + index // subparts + regions - 1, regions),
                "sub": lax.rem(index, subparts),
            },
            device_id_type=MESH,
        )

    def send_cut(index, unused):
        @pl.when(index != subparts + subpart)
        def begin():
            cut_copy(index).start()

        return unused

    lax.fori_loop(0, lists, send_cut, 0)

    def add_terms(inputs, hidden, d_before, d_flux):
        terms[0:wide] += dot(inputs, d_before, 0, 0)
        terms[wide : wide + narrow] += dot(hidden, d_flux, 0, 0)
        bias_terms[0:1] += jnp.sum(d_before.astype(f32), axis=0, keepdims=True)
        bias_terms[1:2] += jnp.sum(d_flux.astype(f32), axis=0, keepdims=True)

    def interior(index, unused):
        at = pl.multiple_of(index * block, 128)
        head_rows = dot(edge_by_cell(edges[0:1, pl.ds(at, block)], cell_count), both[...])
        tail_rows = dot(edge_by_cell(edges[1:2, pl.ds(at, block)], cell_count), both[...])
        inputs, hidden, flux, d_flux, d_before, d_inputs = edge_network(
            head_rows.astype(jnp.bfloat16), tail_rows.astype(jnp.bfloat16), None,
            in_weight[...], in_bias[...], out_weight[...], out_bias[...],
        )
        pieces[index, 0:block, :channels] = flux
        pieces[index, 0:block, channels:] = d_inputs[:, :channels]
        pieces[index, block:, :channels] = -flux
        pieces[index, block:, channels:] = d_inputs[:, channels:]
        add_terms(inputs, hidden, d_before, d_flux)
        return unused

    lax.fori_loop(0, blocks, interior, 0)

    def arrange(index, unused):
        @pl.when(index != subparts + subpart)
        def finish():
            landed_copy(index).wait_recv()

        offset = index // subparts
        peer = lax.rem(region + offset + regions - 1, regions) * subparts + lax.rem(index, subparts)
        lead = jnp.where(me < peer, 1.0, 0.0)
        at = pl.multiple_of(index * slots, 16)
        mask = jnp.full((slots, 2 * channels), lead, f32) > 0.5
        mine, other = own[index].astype(f32), incoming[index].astype(f32)
        heads[pl.ds(at, slots)] = jnp.where(mask, mine, other).astype(jnp.bfloat16)
        tails[pl.ds(at, slots)] = jnp.where(mask, other, mine).astype(jnp.bfloat16)
        slot = lax.broadcasted_iota(jnp.int32, (slots, channels), 0)
        live_rows[pl.ds(at, slots)] = jnp.where(slot < pair_count[index], 1.0, 0.0)
        lead_rows[pl.ds(at, slots)] = jnp.full((slots, channels), lead, f32)
        return unused

    lax.fori_loop(0, lists, arrange, 0)

    def cut(offset, unused):
        at = pl.multiple_of(offset * group, 128)
        rows = pl.ds(at, group)
        live, lead = live_rows[rows], lead_rows[rows]
        inputs, hidden, flux, d_flux, d_before, d_inputs = edge_network(
            heads[rows], tails[rows], live,
            in_weight[...], in_bias[...], out_weight[...], out_bias[...],
        )
        owned = live * lead
        sign = live * (2.0 * lead - 1.0)
        cut_pieces[rows, :channels] = (flux.astype(f32) * sign).astype(jnp.bfloat16)
        spread = d_inputs.astype(f32)
        cut_pieces[rows, channels:] = jnp.where(
            lead > 0.5, spread[:, :channels], spread[:, channels:]
        ).astype(jnp.bfloat16)
        add_terms(
            inputs, hidden,
            (d_before.astype(f32) * owned).astype(jnp.bfloat16),
            (d_flux.astype(f32) * owned).astype(jnp.bfloat16),
        )
        return unused

    lax.fori_loop(0, 3, cut, 0)

    bias_rows = jnp.concatenate(
        [*high_low(bias_terms[0:1]), *high_low(bias_terms[1:2]),
         jnp.zeros((slot_rows - chunk - 4, channels), f32)], axis=0
    )

    def fill(rank, unused):
        part = terms[pl.ds(pl.multiple_of(rank * chunk, 8), chunk)]
        sent[rank] = jnp.concatenate([part, bias_rows], axis=0).astype(jnp.bfloat16)
        return unused

    lax.fori_loop(0, total, fill, 0)
    begin_a, finish_a = exchange(
        me, total, subparts, lambda peer: sent.at[peer], lambda step: landed.at[step], send_a, recv_a
    )
    begin_a()
    landed[0] = sent[me]

    def spread_block(index, unused):
        at = pl.multiple_of(index * block, 128)
        head_table = cell_by_edge(edges[0:1, pl.ds(at, block)], cell_count)
        tail_table = cell_by_edge(edges[1:2, pl.ds(at, block)], cell_count)
        accum[...] += dot(head_table, pieces[index, 0:block]) + dot(tail_table, pieces[index, block:])
        return unused

    accum[...] = dot(cell_by_edge(cut_cells[...], cell_count), cut_pieces[...])
    first = blocks // 2
    lax.fori_loop(0, first, spread_block, 0)
    finish_a()
    owned_sum = jnp.sum(landed[...].astype(f32), axis=0)
    gathered[me] = owned_sum.astype(jnp.bfloat16)
    begin_b, finish_b = exchange(
        me, total, subparts, lambda peer: gathered.at[me], lambda step: gathered.at[me], send_b, recv_b
    )
    begin_b()
    lax.fori_loop(first, blocks, spread_block, 0)
    in_bias_out[...] = normalized(owned_sum[chunk : chunk + 1] + owned_sum[chunk + 1 : chunk + 2])
    out_bias_out[...] = normalized(owned_sum[chunk + 2 : chunk + 3] + owned_sum[chunk + 3 : chunk + 4])
    new_latents[...] = (latents[...].astype(f32) + accum[:, :channels]).astype(jnp.bfloat16)
    latent_grad[...] = (cotangent[...].astype(f32) + accum[:, channels:]).astype(jnp.bfloat16)

    def sent_cut(index, unused):
        @pl.when(index != subparts + subpart)
        def finish():
            landed_copy(index).wait_send()

        return unused

    lax.fori_loop(0, lists, sent_cut, 0)
    finish_b()
    everything = gathered[...].astype(f32)[:, :chunk].reshape(total * chunk, channels)
    in_weight_out[...] = normalized(everything[:wide])
    out_weight_out[...] = normalized(everything[wide : wide + narrow])


def hand_on(*refs):
    sources, targets, done = refs[:6], refs[6:12], refs[12]
    copies = [
        pltpu.make_async_copy(source, target, done.at[place])
        for place, (source, target) in enumerate(zip(sources, targets))
    ]
    for copy in copies:
        copy.start()
    for copy in copies:
        copy.wait()


def local(
    latents, cotangent, inner_edges, cut_cells, pair_count, in_weight, in_bias, out_weight, out_bias
):
    regions = lax.axis_size("region")
    subparts = lax.axis_size("sub")
    total = regions * subparts
    cell_count, channels = latents.shape
    edge_total = inner_edges.shape[1]
    wide, hidden = in_weight.shape
    narrow = out_weight.shape[0]
    lists = pair_count.shape[0]
    slots = cut_cells.shape[0] // lists
    cut_total = lists * slots
    block = 1024
    blocks = edge_total // block
    chunk = round_up(-(-(wide + narrow) // total), 8)
    slot_rows = round_up(chunk + 4, 16)
    vmem = pl.BlockSpec(memory_space=pltpu.VMEM)
    hbm = pl.BlockSpec(memory_space=pl.ANY)
    smem = pl.BlockSpec(memory_space=pltpu.SMEM)
    f32, bf16 = jnp.float32, jnp.bfloat16
    dma = pltpu.SemaphoreType.DMA
    results = pl.pallas_call(
        functools.partial(layer_kernel, regions, subparts, chunk, block),
        out_shape=[
            jax.ShapeDtypeStruct((cell_count, channels), bf16),
            jax.ShapeDtypeStruct((cell_count, channels), bf16),
            jax.ShapeDtypeStruct((wide, hidden), f32),
            jax.ShapeDtypeStruct((1, hidden), f32),
            jax.ShapeDtypeStruct((narrow, channels), f32),
            jax.ShapeDtypeStruct((1, channels), f32),
        ],
        in_specs=[hbm, hbm, hbm, vmem, smem, hbm, vmem, hbm, vmem],
        out_specs=[vmem] * 6,
        scratch_shapes=[
            pltpu.VMEM((cell_count, channels), bf16),
            pltpu.VMEM((cell_count, channels), bf16),
            pltpu.VMEM((2, edge_total), jnp.int32),
            pltpu.VMEM((1, cut_total), jnp.int32),
            pltpu.VMEM((wide, hidden), bf16),
            pltpu.VMEM((narrow, channels), bf16),
            dma((5,)),
            pltpu.VMEM((cell_count, 2 * channels), bf16),
            pltpu.VMEM((lists, slots, 2 * channels), bf16),
            pltpu.VMEM((lists, slots, 2 * channels), bf16),
            pltpu.VMEM((cut_total, 2 * channels), bf16),
            pltpu.VMEM((cut_total, 2 * channels), bf16),
            pltpu.VMEM((cut_total, channels), f32),
            pltpu.VMEM((cut_total, channels), f32),
            pltpu.VMEM((blocks, 2 * block, 2 * channels), bf16),
            pltpu.VMEM((cut_total, 2 * channels), bf16),
            pltpu.VMEM((cell_count, 2 * channels), f32),
            pltpu.VMEM((max(total * chunk, wide + narrow), channels), f32),
            pltpu.VMEM((8, channels), f32),
            pltpu.VMEM((total, slot_rows, channels), bf16),
            pltpu.VMEM((total, slot_rows, channels), bf16),
            pltpu.VMEM((total, slot_rows, channels), bf16),
            dma((lists,)),
            dma((lists,)),
            dma((total,)),
            dma((total,)),
            dma((total,)),
            dma((total,)),
        ],
        compiler_params=pltpu.CompilerParams(
            collective_id=0, has_side_effects=True, vmem_limit_bytes=60 * 1024 * 1024
        ),
    )(
        latents, cotangent, inner_edges, cut_cells, pair_count,
        in_weight, in_bias[None], out_weight, out_bias[None],
    )
    a, b, c, d, e, f = pl.pallas_call(
        hand_on,
        out_shape=[jax.ShapeDtypeStruct(result.shape, result.dtype) for result in results],
        in_specs=[hbm] * 6,
        out_specs=[hbm] * 6,
        scratch_shapes=[dma((6,))],
        compiler_params=pltpu.CompilerParams(vmem_limit_bytes=60 * 1024 * 1024),
    )(*results)
    return a, b, c, d[0], e, f[0]


def solution(mesh):
    placed = (
        P(("groups", "region", "sub"), None),
        P(("groups", "region", "sub"), None),
        P(None, ("groups", "region", "sub")),
        P(("groups", "region", "sub")),
        P(("groups", "region", "sub")),
        P(),
        P(),
        P(),
        P(),
    )
    return jax.shard_map(
        local,
        mesh=mesh,
        in_specs=placed,
        out_specs=(
            P(("groups", "region", "sub"), None),
            P(("groups", "region", "sub"), None),
            P("groups", None),
            P("groups"),
            P("groups", None),
            P("groups"),
        ),
        check_vma=False,
    )
```

```python
import functools

import jax
import jax.numpy as jnp
from jax import lax
from jax.experimental import pallas as pl
from jax.experimental.pallas import tpu as pltpu
from jax.sharding import PartitionSpec as P

MESH = pl.DeviceIdType.MESH


def round_up(value, step):
    return -(-value // step) * step


def device_at(rank, subparts):
    return {"region": lax.div(rank, jnp.int32(subparts)), "sub": lax.rem(rank, subparts)}


def high_low(value):
    high = value.astype(jnp.bfloat16).astype(jnp.float32)
    return high, value - high


def exchange(me, total, subparts, source, target, send_sem, recv_sem):
    def copy_of(step):
        peer = lax.rem(me + step, total)
        return pltpu.make_async_remote_copy(
            src_ref=source(peer),
            dst_ref=target(step),
            send_sem=send_sem.at[step],
            recv_sem=recv_sem.at[step],
            device_id=device_at(peer, subparts),
            device_id_type=MESH,
        )

    def begin(step, unused):
        copy_of(step).start()
        return unused

    def finish(step, unused):
        copy_of(step).wait()
        return unused

    return (
        lambda: lax.fori_loop(1, total, begin, 0),
        lambda: lax.fori_loop(1, total, finish, 0),
    )


def normalized(gradient):
    return gradient / jnp.sqrt(jnp.mean(gradient * gradient) + 1e-06)


def dot(left, right, left_axis=1, right_axis=0):
    return lax.dot_general(
        left, right, (((left_axis,), (right_axis,)), ((), ())), preferred_element_type=jnp.float32
    )


def edge_by_cell(cell_row, cell_count):
    rows = cell_row.shape[1]
    spread = jnp.transpose(jnp.broadcast_to(cell_row, (128, rows)))
    lane = lax.broadcasted_iota(jnp.int32, (rows, 128), 1)
    low = jnp.where(spread & 127 == lane, 1.0, 0.0).astype(jnp.bfloat16)
    high = (lax.shift_right_logical(spread, 7)).astype(jnp.float32).astype(jnp.bfloat16)
    zero = jnp.zeros((rows, 128), jnp.bfloat16)
    return jnp.concatenate(
        [jnp.where(high == jnp.bfloat16(part), low, zero) for part in range(cell_count // 128)], axis=1
    )


def cell_by_edge(cell_row, cell_count):
    rows = cell_row.shape[1]
    spread = jnp.broadcast_to(cell_row, (16, rows))
    cell = lax.broadcasted_iota(jnp.int32, (16, rows), 0)
    low = jnp.where(spread & 15 == cell, 1.0, 0.0).astype(jnp.bfloat16)
    high = (lax.shift_right_logical(spread, 4)).astype(jnp.float32).astype(jnp.bfloat16)
    zero = jnp.zeros((16, rows), jnp.bfloat16)
    return jnp.concatenate(
        [jnp.where(high == jnp.bfloat16(part), low, zero) for part in range(cell_count // 16)], axis=0
    )


def edge_network(head_rows, tail_rows, live, in_weight, in_bias, out_weight, out_bias):
    channels = out_weight.shape[1]
    inputs = jnp.concatenate([head_rows[:, :channels], tail_rows[:, :channels]], axis=1)
    before = dot(inputs, in_weight) + in_bias
    logistic = 1.0 / (1.0 + jnp.exp(-before))
    hidden = (before * logistic).astype(jnp.bfloat16)
    flux = (dot(hidden, out_weight) + out_bias).astype(jnp.bfloat16)
    d_flux = head_rows[:, channels:].astype(jnp.float32) - tail_rows[:, channels:].astype(jnp.float32)
    if live is not None:
        d_flux = d_flux * live
    d_flux = d_flux.astype(jnp.bfloat16)
    d_hidden = dot(d_flux, out_weight, 1, 1)
    d_before = (d_hidden * logistic * (1.0 + before * (1.0 - logistic))).astype(jnp.bfloat16)
    d_inputs = dot(d_before, in_weight, 1, 1).astype(jnp.bfloat16)
    return inputs, hidden, flux, d_flux, d_before, d_inputs


def layer_kernel(
    regions, subparts, chunk, block,
    latents_from, cotangent_from, edges_from, cut_flat, pair_count, in_weight_from, in_bias, out_weight_from, out_bias,
    new_latents, latent_grad, in_weight_out, in_bias_out, out_weight_out, out_bias_out,
    latents, cotangent, edges, cut_cells, in_weight, out_weight, arrived,
    both, own, incoming, heads, tails, live_rows, lead_rows, pieces, cut_pieces, accum,
    terms, wide_terms, bias_terms, sent, landed, gathered,
    cut_send, cut_recv, send_a, recv_a, send_b, recv_b,
):
    total = regions * subparts
    region = lax.axis_index("region")
    subpart = lax.axis_index("sub")
    me = region * subparts + subpart
    cell_count, channels = latents.shape
    wide = in_weight.shape[0]
    narrow = out_weight.shape[0]
    slot_rows = sent.shape[1]
    lists, slots = own.shape[0], own.shape[1]
    blocks = edges.shape[1] // block
    f32 = jnp.float32

    fetches = [
        pltpu.make_async_copy(source, target, arrived.at[place])
        for place, (source, target) in enumerate(
            (
                (latents_from, latents),
                (cotangent_from, cotangent),
                (edges_from, edges),
                (in_weight_from, in_weight),
                (out_weight_from, out_weight),
            )
        )
    ]
    for fetch in fetches:
        fetch.start()
    barrier = pltpu.get_barrier_semaphore()

    def greet(step, unused):
        peer = lax.rem(me + step, total)
        pl.semaphore_signal(barrier, inc=1, device_id=device_at(peer, subparts), device_id_type=MESH)
        return unused

    lax.fori_loop(1, total, greet, 0)

    cut_cells[...] = cut_flat[...].reshape(1, -1)
    for fetch in fetches:
        fetch.wait()
    both[:, :channels] = latents[...]
    both[:, channels:] = cotangent[...]
    terms[...] = jnp.zeros(terms.shape, f32)
    wide_terms[...] = jnp.zeros(wide_terms.shape, f32)
    bias_terms[...] = jnp.zeros(bias_terms.shape, f32)
    group = subparts * slots

    def pick_cut(offset, unused):
        at = pl.multiple_of(offset * group, 128)
        table = edge_by_cell(cut_cells[:, pl.ds(at, group)], cell_count)
        rows = dot(table, both[...]).astype(jnp.bfloat16)
        own[pl.ds(offset * subparts, subparts)] = rows.reshape(subparts, slots, 2 * channels)
        return unused

    lax.fori_loop(0, 3, pick_cut, 0)
    incoming[subparts + subpart] = jnp.zeros((slots, 2 * channels), jnp.bfloat16)
    pl.semaphore_wait(barrier, total - 1)

    def cut_copy(index):
        offset = index // subparts
        other = lax.rem(index, subparts)
        there = (2 - offset) * subparts + subpart
        return pltpu.make_async_remote_copy(
            src_ref=own.at[index],
            dst_ref=incoming.at[there],
            send_sem=cut_send.at[index],
            recv_sem=cut_recv.at[there],
            device_id={"region": lax.rem(region + offset + regions - 1, regions), "sub": other},
            device_id_type=MESH,
        )

    def landed_copy(index):
        return pltpu.make_async_remote_copy(
            src_ref=own.at[index],
            dst_ref=incoming.at[index],
            send_sem=cut_send.at[index],
            recv_sem=cut_recv.at[index],
            device_id={
                "region": lax.rem(region + index // subparts + regions - 1, regions),
                "sub": lax.rem(index, subparts),
            },
            device_id_type=MESH,
        )

    def send_cut(index, unused):
        @pl.when(index != subparts + subpart)
        def begin():
            cut_copy(index).start()

        return unused

    lax.fori_loop(0, lists, send_cut, 0)

    def add_terms(inputs, hidden, d_before, d_flux):
        wide_terms[...] += dot(d_before, inputs, 0, 0)
        terms[wide : wide + narrow] += dot(hidden, d_flux, 0, 0)
        bias_terms[0:1] += jnp.sum(d_before.astype(f32), axis=0, keepdims=True)
        bias_terms[1:2] += jnp.sum(d_flux.astype(f32), axis=0, keepdims=True)

    def interior(index, unused):
        at = pl.multiple_of(index * block, 128)
        head_rows = dot(edge_by_cell(edges[0:1, pl.ds(at, block)], cell_count), both[...])
        tail_rows = dot(edge_by_cell(edges[1:2, pl.ds(at, block)], cell_count), both[...])
        inputs, hidden, flux, d_flux, d_before, d_inputs = edge_network(
            head_rows.astype(jnp.bfloat16), tail_rows.astype(jnp.bfloat16), None,
            in_weight[...], in_bias[...], out_weight[...], out_bias[...],
        )
        pieces[index, 0:block, :channels] = flux
        pieces[index, 0:block, channels:] = d_inputs[:, :channels]
        pieces[index, block:, :channels] = -flux
        pieces[index, block:, channels:] = d_inputs[:, channels:]
        add_terms(inputs, hidden, d_before, d_flux)
        return unused

    lax.fori_loop(0, blocks, interior, 0, unroll=True)

    def arrange(index, unused):
        @pl.when(index != subparts + subpart)
        def finish():
            landed_copy(index).wait_recv()

        offset = index // subparts
        peer = lax.rem(region + offset + regions - 1, regions) * subparts + lax.rem(index, subparts)
        lead = jnp.where(me < peer, 1.0, 0.0)
        at = pl.multiple_of(index * slots, 16)
        mask = jnp.full((slots, 2 * channels), lead, f32) > 0.5
        mine, other = own[index].astype(f32), incoming[index].astype(f32)
        heads[pl.ds(at, slots)] = jnp.where(mask, mine, other).astype(jnp.bfloat16)
        tails[pl.ds(at, slots)] = jnp.where(mask, other, mine).astype(jnp.bfloat16)
        slot = lax.broadcasted_iota(jnp.int32, (slots, channels), 0)
        live_rows[pl.ds(at, slots)] = jnp.where(slot < pair_count[index], 1.0, 0.0)
        lead_rows[pl.ds(at, slots)] = jnp.full((slots, channels), lead, f32)
        return unused

    lax.fori_loop(0, lists, arrange, 0)

    def cut(offset, unused):
        at = pl.multiple_of(offset * group, 128)
        rows = pl.ds(at, group)
        live, lead = live_rows[rows], lead_rows[rows]
        inputs, hidden, flux, d_flux, d_before, d_inputs = edge_network(
            heads[rows], tails[rows], live,
            in_weight[...], in_bias[...], out_weight[...], out_bias[...],
        )
        owned = live * lead
        sign = live * (2.0 * lead - 1.0)
        cut_pieces[rows, :channels] = (flux.astype(f32) * sign).astype(jnp.bfloat16)
        spread = d_inputs.astype(f32)
        cut_pieces[rows, channels:] = jnp.where(
            lead > 0.5, spread[:, :channels], spread[:, channels:]
        ).astype(jnp.bfloat16)
        add_terms(
            inputs, hidden,
            (d_before.astype(f32) * owned).astype(jnp.bfloat16),
            (d_flux.astype(f32) * owned).astype(jnp.bfloat16),
        )
        return unused

    lax.fori_loop(0, 3, cut, 0)

    terms[0:wide] = jnp.transpose(wide_terms[...])
    bias_rows = jnp.concatenate(
        [*high_low(bias_terms[0:1]), *high_low(bias_terms[1:2]),
         jnp.zeros((slot_rows - chunk - 4, channels), f32)], axis=0
    )

    def fill(rank, unused):
        part = terms[pl.ds(pl.multiple_of(rank * chunk, 8), chunk)]
        sent[rank] = jnp.concatenate([part, bias_rows], axis=0).astype(jnp.bfloat16)
        return unused

    lax.fori_loop(0, total, fill, 0)
    begin_a, finish_a = exchange(
        me, total, subparts, lambda peer: sent.at[peer], lambda step: landed.at[step], send_a, recv_a
    )
    begin_a()
    landed[0] = sent[me]

    def spread_block(index, unused):
        at = pl.multiple_of(index * block, 128)
        head_table = cell_by_edge(edges[0:1, pl.ds(at, block)], cell_count)
        tail_table = cell_by_edge(edges[1:2, pl.ds(at, block)], cell_count)
        accum[...] += dot(head_table, pieces[index, 0:block]) + dot(tail_table, pieces[index, block:])
        return unused

    accum[...] = dot(cell_by_edge(cut_cells[...], cell_count), cut_pieces[...])
    first = blocks // 2
    lax.fori_loop(0, first, spread_block, 0)
    finish_a()
    owned_sum = jnp.sum(landed[...].astype(f32), axis=0)
    gathered[me] = owned_sum.astype(jnp.bfloat16)
    begin_b, finish_b = exchange(
        me, total, subparts, lambda peer: gathered.at[me], lambda step: gathered.at[me], send_b, recv_b
    )
    begin_b()
    lax.fori_loop(first, blocks, spread_block, 0, unroll=True)
    in_bias_out[...] = normalized(owned_sum[chunk : chunk + 1] + owned_sum[chunk + 1 : chunk + 2])
    out_bias_out[...] = normalized(owned_sum[chunk + 2 : chunk + 3] + owned_sum[chunk + 3 : chunk + 4])
    new_latents[...] = (latents[...].astype(f32) + accum[:, :channels]).astype(jnp.bfloat16)
    latent_grad[...] = (cotangent[...].astype(f32) + accum[:, channels:]).astype(jnp.bfloat16)

    def sent_cut(index, unused):
        @pl.when(index != subparts + subpart)
        def finish():
            landed_copy(index).wait_send()

        return unused

    lax.fori_loop(0, lists, sent_cut, 0)
    finish_b()
    everything = gathered[...].astype(f32)[:, :chunk].reshape(total * chunk, channels)
    in_weight_out[...] = normalized(everything[:wide])
    out_weight_out[...] = normalized(everything[wide : wide + narrow])


def hand_on(*refs):
    sources, targets, held = refs[:6], refs[6:12], refs[12:18]
    came, left = refs[18], refs[19]
    fetches = [
        pltpu.make_async_copy(source, target, came.at[place])
        for place, (source, target) in enumerate(zip(sources, held))
    ]
    writes = [
        pltpu.make_async_copy(source, target, left.at[place])
        for place, (source, target) in enumerate(zip(held, targets))
    ]
    for fetch in fetches:
        fetch.start()
    for fetch, write in zip(fetches, writes):
        fetch.wait()
        write.start()
    for write in writes:
        write.wait()


def local(
    latents, cotangent, inner_edges, cut_cells, pair_count, in_weight, in_bias, out_weight, out_bias
):
    regions = lax.axis_size("region")
    subparts = lax.axis_size("sub")
    total = regions * subparts
    cell_count, channels = latents.shape
    edge_total = inner_edges.shape[1]
    wide, hidden = in_weight.shape
    narrow = out_weight.shape[0]
    lists = pair_count.shape[0]
    slots = cut_cells.shape[0] // lists
    cut_total = lists * slots
    block = 1024
    blocks = edge_total // block
    chunk = round_up(-(-(wide + narrow) // total), 8)
    slot_rows = round_up(chunk + 4, 16)
    vmem = pl.BlockSpec(memory_space=pltpu.VMEM)
    hbm = pl.BlockSpec(memory_space=pl.ANY)
    smem = pl.BlockSpec(memory_space=pltpu.SMEM)
    f32, bf16 = jnp.float32, jnp.bfloat16
    dma = pltpu.SemaphoreType.DMA
    results = pl.pallas_call(
        functools.partial(layer_kernel, regions, subparts, chunk, block),
        out_shape=[
            jax.ShapeDtypeStruct((cell_count, channels), bf16),
            jax.ShapeDtypeStruct((cell_count, channels), bf16),
            jax.ShapeDtypeStruct((wide, hidden), f32),
            jax.ShapeDtypeStruct((1, hidden), f32),
            jax.ShapeDtypeStruct((narrow, channels), f32),
            jax.ShapeDtypeStruct((1, channels), f32),
        ],
        in_specs=[hbm, hbm, hbm, vmem, smem, hbm, vmem, hbm, vmem],
        out_specs=[vmem] * 6,
        scratch_shapes=[
            pltpu.VMEM((cell_count, channels), bf16),
            pltpu.VMEM((cell_count, channels), bf16),
            pltpu.VMEM((2, edge_total), jnp.int32),
            pltpu.VMEM((1, cut_total), jnp.int32),
            pltpu.VMEM((wide, hidden), bf16),
            pltpu.VMEM((narrow, channels), bf16),
            dma((5,)),
            pltpu.VMEM((cell_count, 2 * channels), bf16),
            pltpu.VMEM((lists, slots, 2 * channels), bf16),
            pltpu.VMEM((lists, slots, 2 * channels), bf16),
            pltpu.VMEM((cut_total, 2 * channels), bf16),
            pltpu.VMEM((cut_total, 2 * channels), bf16),
            pltpu.VMEM((cut_total, channels), f32),
            pltpu.VMEM((cut_total, channels), f32),
            pltpu.VMEM((blocks, 2 * block, 2 * channels), bf16),
            pltpu.VMEM((cut_total, 2 * channels), bf16),
            pltpu.VMEM((cell_count, 2 * channels), f32),
            pltpu.VMEM((max(total * chunk, wide + narrow), channels), f32),
            pltpu.VMEM((hidden, wide), f32),
            pltpu.VMEM((8, channels), f32),
            pltpu.VMEM((total, slot_rows, channels), bf16),
            pltpu.VMEM((total, slot_rows, channels), bf16),
            pltpu.VMEM((total, slot_rows, channels), bf16),
            dma((lists,)),
            dma((lists,)),
            dma((total,)),
            dma((total,)),
            dma((total,)),
            dma((total,)),
        ],
        compiler_params=pltpu.CompilerParams(
            collective_id=0, has_side_effects=True, vmem_limit_bytes=60 * 1024 * 1024
        ),
    )(
        latents, cotangent, inner_edges, cut_cells, pair_count,
        in_weight, in_bias[None], out_weight, out_bias[None],
    )
    a, b, c, d, e, f = pl.pallas_call(
        hand_on,
        out_shape=[jax.ShapeDtypeStruct(result.shape, result.dtype) for result in results],
        in_specs=[hbm] * 6,
        out_specs=[hbm] * 6,
        scratch_shapes=[*(pltpu.VMEM(result.shape, result.dtype) for result in results), dma((6,)), dma((6,))],
        compiler_params=pltpu.CompilerParams(vmem_limit_bytes=60 * 1024 * 1024),
    )(*results)
    return a, b, c, d[0], e, f[0]


def solution(mesh):
    placed = (
        P(("groups", "region", "sub"), None),
        P(("groups", "region", "sub"), None),
        P(None, ("groups", "region", "sub")),
        P(("groups", "region", "sub")),
        P(("groups", "region", "sub")),
        P(),
        P(),
        P(),
        P(),
    )
    return jax.shard_map(
        local,
        mesh=mesh,
        in_specs=placed,
        out_specs=(
            P(("groups", "region", "sub"), None),
            P(("groups", "region", "sub"), None),
            P("groups", None),
            P("groups"),
            P("groups", None),
            P("groups"),
        ),
        check_vma=False,
    )
```

```python
import functools

import jax
import jax.numpy as jnp
from jax import lax
from jax.experimental import pallas as pl
from jax.experimental.pallas import tpu as pltpu
from jax.sharding import PartitionSpec as P

MESH = pl.DeviceIdType.MESH


def round_up(value, step):
    return -(-value // step) * step


def device_at(rank, subparts):
    return {"region": lax.div(rank, jnp.int32(subparts)), "sub": lax.rem(rank, subparts)}


def high_low(value):
    high = value.astype(jnp.bfloat16).astype(jnp.float32)
    return high, value - high


def exchange(me, total, subparts, source, target, send_sem, recv_sem):
    def copy_of(step):
        peer = lax.rem(me + step, total)
        return pltpu.make_async_remote_copy(
            src_ref=source(peer),
            dst_ref=target(step),
            send_sem=send_sem.at[step],
            recv_sem=recv_sem.at[step],
            device_id=device_at(peer, subparts),
            device_id_type=MESH,
        )

    def begin(step, unused):
        copy_of(step).start()
        return unused

    def finish(step, unused):
        copy_of(step).wait()
        return unused

    return (
        lambda: lax.fori_loop(1, total, begin, 0),
        lambda: lax.fori_loop(1, total, finish, 0),
    )


def normalized(gradient):
    return gradient / jnp.sqrt(jnp.mean(gradient * gradient) + 1e-06)


def dot(left, right, left_axis=1, right_axis=0):
    return lax.dot_general(
        left, right, (((left_axis,), (right_axis,)), ((), ())), preferred_element_type=jnp.float32
    )


def edge_by_cell(cell_row, cell_count):
    rows = cell_row.shape[1]
    spread = jnp.transpose(jnp.broadcast_to(cell_row, (128, rows)))
    lane = lax.broadcasted_iota(jnp.int32, (rows, 128), 1)
    low = jnp.where(spread & 127 == lane, 1.0, 0.0).astype(jnp.bfloat16)
    high = (lax.shift_right_logical(spread, 7)).astype(jnp.float32).astype(jnp.bfloat16)
    zero = jnp.zeros((rows, 128), jnp.bfloat16)
    return jnp.concatenate(
        [jnp.where(high == jnp.bfloat16(part), low, zero) for part in range(cell_count // 128)], axis=1
    )


def cell_by_edge(cell_row, cell_count):
    rows = cell_row.shape[1]
    spread = jnp.broadcast_to(cell_row, (16, rows))
    cell = lax.broadcasted_iota(jnp.int32, (16, rows), 0)
    low = jnp.where(spread & 15 == cell, 1.0, 0.0).astype(jnp.bfloat16)
    high = (lax.shift_right_logical(spread, 4)).astype(jnp.float32).astype(jnp.bfloat16)
    zero = jnp.zeros((16, rows), jnp.bfloat16)
    return jnp.concatenate(
        [jnp.where(high == jnp.bfloat16(part), low, zero) for part in range(cell_count // 16)], axis=0
    )


def edge_network(head_rows, tail_rows, live, in_weight, in_bias, out_weight, out_bias):
    channels = out_weight.shape[1]
    inputs = jnp.concatenate([head_rows[:, :channels], tail_rows[:, :channels]], axis=1)
    before = dot(inputs, in_weight) + in_bias
    logistic = 1.0 / (1.0 + jnp.exp(-before))
    hidden = (before * logistic).astype(jnp.bfloat16)
    flux = (dot(hidden, out_weight) + out_bias).astype(jnp.bfloat16)
    d_flux = head_rows[:, channels:].astype(jnp.float32) - tail_rows[:, channels:].astype(jnp.float32)
    if live is not None:
        d_flux = d_flux * live
    d_flux = d_flux.astype(jnp.bfloat16)
    d_hidden = dot(d_flux, out_weight, 1, 1)
    d_before = (d_hidden * logistic * (1.0 + before * (1.0 - logistic))).astype(jnp.bfloat16)
    d_inputs = dot(d_before, in_weight, 1, 1).astype(jnp.bfloat16)
    return inputs, hidden, flux, d_flux, d_before, d_inputs


def layer_kernel(
    regions, subparts, chunk, block,
    latents_from, cotangent_from, edges_from, cut_flat, pair_count, in_weight_from, in_bias, out_weight_from, out_bias,
    new_latents, latent_grad, in_weight_out, in_bias_out, out_weight_out, out_bias_out,
    latents, cotangent, edges, cut_cells, in_weight, out_weight, arrived,
    both, own, incoming, heads, tails, live_rows, lead_rows, pieces, cut_pieces, accum,
    terms, wide_terms, bias_terms, sent, landed, gathered,
    cut_send, cut_recv, send_a, recv_a, send_b, recv_b,
):
    total = regions * subparts
    region = lax.axis_index("region")
    subpart = lax.axis_index("sub")
    me = region * subparts + subpart
    cell_count, channels = latents.shape
    wide = in_weight.shape[0]
    narrow = out_weight.shape[0]
    slot_rows = sent.shape[1]
    lists, slots = own.shape[0], own.shape[1]
    blocks = edges.shape[1] // block
    f32 = jnp.float32

    fetches = [
        pltpu.make_async_copy(source, target, arrived.at[place])
        for place, (source, target) in enumerate(
            (
                (latents_from, latents),
                (cotangent_from, cotangent),
                (edges_from, edges),
                (in_weight_from, in_weight),
                (out_weight_from, out_weight),
            )
        )
    ]
    for fetch in fetches:
        fetch.start()
    barrier = pltpu.get_barrier_semaphore()

    def greet(step, unused):
        peer = lax.rem(me + step, total)
        pl.semaphore_signal(barrier, inc=1, device_id=device_at(peer, subparts), device_id_type=MESH)
        return unused

    lax.fori_loop(1, total, greet, 0)

    cut_cells[...] = cut_flat[...].reshape(1, -1)
    for fetch in fetches:
        fetch.wait()
    both[:, :channels] = latents[...]
    both[:, channels:] = cotangent[...]
    terms[...] = jnp.zeros(terms.shape, f32)
    wide_terms[...] = jnp.zeros(wide_terms.shape, f32)
    bias_terms[...] = jnp.zeros(bias_terms.shape, f32)
    group = lists * slots

    cut_table = edge_by_cell(cut_cells[...], cell_count)
    own[...] = dot(cut_table, both[...]).astype(jnp.bfloat16).reshape(lists, slots, 2 * channels)
    incoming[subparts + subpart] = jnp.zeros((slots, 2 * channels), jnp.bfloat16)
    pl.semaphore_wait(barrier, total - 1)

    def cut_copy(index):
        offset = index // subparts
        other = lax.rem(index, subparts)
        there = (2 - offset) * subparts + subpart
        return pltpu.make_async_remote_copy(
            src_ref=own.at[index],
            dst_ref=incoming.at[there],
            send_sem=cut_send.at[index],
            recv_sem=cut_recv.at[there],
            device_id={"region": lax.rem(region + offset + regions - 1, regions), "sub": other},
            device_id_type=MESH,
        )

    def landed_copy(index):
        return pltpu.make_async_remote_copy(
            src_ref=own.at[index],
            dst_ref=incoming.at[index],
            send_sem=cut_send.at[index],
            recv_sem=cut_recv.at[index],
            device_id={
                "region": lax.rem(region + index // subparts + regions - 1, regions),
                "sub": lax.rem(index, subparts),
            },
            device_id_type=MESH,
        )

    def send_cut(index, unused):
        @pl.when(index != subparts + subpart)
        def begin():
            cut_copy(index).start()

        return unused

    lax.fori_loop(0, lists, send_cut, 0)

    def add_terms(inputs, hidden, d_before, d_flux):
        wide_terms[...] += dot(d_before, inputs, 0, 0)
        terms[wide : wide + narrow] += dot(hidden, d_flux, 0, 0)
        bias_terms[0:1] += jnp.sum(d_before.astype(f32), axis=0, keepdims=True)
        bias_terms[1:2] += jnp.sum(d_flux.astype(f32), axis=0, keepdims=True)

    def interior(index, unused):
        at = pl.multiple_of(index * block, 128)
        head_rows = dot(edge_by_cell(edges[0:1, pl.ds(at, block)], cell_count), both[...])
        tail_rows = dot(edge_by_cell(edges[1:2, pl.ds(at, block)], cell_count), both[...])
        inputs, hidden, flux, d_flux, d_before, d_inputs = edge_network(
            head_rows.astype(jnp.bfloat16), tail_rows.astype(jnp.bfloat16), None,
            in_weight[...], in_bias[...], out_weight[...], out_bias[...],
        )
        pieces[index, 0:block, :channels] = flux
        pieces[index, 0:block, channels:] = d_inputs[:, :channels]
        pieces[index, block:, :channels] = -flux
        pieces[index, block:, channels:] = d_inputs[:, channels:]
        add_terms(inputs, hidden, d_before, d_flux)
        return unused

    lax.fori_loop(0, blocks, interior, 0, unroll=True)

    def arrange(index, unused):
        @pl.when(index != subparts + subpart)
        def finish():
            landed_copy(index).wait_recv()

        offset = index // subparts
        peer = lax.rem(region + offset + regions - 1, regions) * subparts + lax.rem(index, subparts)
        lead = jnp.where(me < peer, 1.0, 0.0)
        at = pl.multiple_of(index * slots, 16)
        mask = jnp.full((slots, 2 * channels), lead, f32) > 0.5
        mine, other = own[index].astype(f32), incoming[index].astype(f32)
        heads[pl.ds(at, slots)] = jnp.where(mask, mine, other).astype(jnp.bfloat16)
        tails[pl.ds(at, slots)] = jnp.where(mask, other, mine).astype(jnp.bfloat16)
        slot = lax.broadcasted_iota(jnp.int32, (slots, channels), 0)
        live_rows[pl.ds(at, slots)] = jnp.where(slot < pair_count[index], 1.0, 0.0)
        lead_rows[pl.ds(at, slots)] = jnp.full((slots, channels), lead, f32)
        return unused

    lax.fori_loop(0, lists, arrange, 0)

    def cut():
        rows = pl.ds(0, group)
        live, lead = live_rows[rows], lead_rows[rows]
        inputs, hidden, flux, d_flux, d_before, d_inputs = edge_network(
            heads[rows], tails[rows], live,
            in_weight[...], in_bias[...], out_weight[...], out_bias[...],
        )
        owned = live * lead
        sign = live * (2.0 * lead - 1.0)
        cut_pieces[rows, :channels] = (flux.astype(f32) * sign).astype(jnp.bfloat16)
        spread = d_inputs.astype(f32)
        cut_pieces[rows, channels:] = jnp.where(
            lead > 0.5, spread[:, :channels], spread[:, channels:]
        ).astype(jnp.bfloat16)
        add_terms(
            inputs, hidden,
            (d_before.astype(f32) * owned).astype(jnp.bfloat16),
            (d_flux.astype(f32) * owned).astype(jnp.bfloat16),
        )

    cut()

    terms[0:wide] = jnp.transpose(wide_terms[...])
    bias_rows = jnp.concatenate(
        [*high_low(bias_terms[0:1]), *high_low(bias_terms[1:2]),
         jnp.zeros((slot_rows - chunk - 4, channels), f32)], axis=0
    )

    def fill(rank, unused):
        part = terms[pl.ds(pl.multiple_of(rank * chunk, 8), chunk)]
        sent[rank] = jnp.concatenate([part, bias_rows], axis=0).astype(jnp.bfloat16)
        return unused

    lax.fori_loop(0, total, fill, 0)
    begin_a, finish_a = exchange(
        me, total, subparts, lambda peer: sent.at[peer], lambda step: landed.at[step], send_a, recv_a
    )
    begin_a()
    landed[0] = sent[me]

    def spread_block(index, unused):
        at = pl.multiple_of(index * block, 128)
        head_table = cell_by_edge(edges[0:1, pl.ds(at, block)], cell_count)
        tail_table = cell_by_edge(edges[1:2, pl.ds(at, block)], cell_count)
        accum[...] += dot(head_table, pieces[index, 0:block]) + dot(tail_table, pieces[index, block:])
        return unused

    accum[...] = dot(cell_by_edge(cut_cells[...], cell_count), cut_pieces[...])
    first = blocks // 2
    lax.fori_loop(0, first, spread_block, 0)
    finish_a()
    owned_sum = jnp.sum(landed[...].astype(f32), axis=0)
    gathered[me] = owned_sum.astype(jnp.bfloat16)
    begin_b, finish_b = exchange(
        me, total, subparts, lambda peer: gathered.at[me], lambda step: gathered.at[me], send_b, recv_b
    )
    begin_b()
    lax.fori_loop(first, blocks, spread_block, 0, unroll=True)
    in_bias_out[...] = normalized(owned_sum[chunk : chunk + 1] + owned_sum[chunk + 1 : chunk + 2])
    out_bias_out[...] = normalized(owned_sum[chunk + 2 : chunk + 3] + owned_sum[chunk + 3 : chunk + 4])
    new_latents[...] = (latents[...].astype(f32) + accum[:, :channels]).astype(jnp.bfloat16)
    latent_grad[...] = (cotangent[...].astype(f32) + accum[:, channels:]).astype(jnp.bfloat16)

    def sent_cut(index, unused):
        @pl.when(index != subparts + subpart)
        def finish():
            landed_copy(index).wait_send()

        return unused

    lax.fori_loop(0, lists, sent_cut, 0)
    finish_b()
    everything = gathered[...].astype(f32)[:, :chunk].reshape(total * chunk, channels)
    in_weight_out[...] = normalized(everything[:wide])
    out_weight_out[...] = normalized(everything[wide : wide + narrow])


def hand_on(*refs):
    sources, targets, held = refs[:6], refs[6:12], refs[12:18]
    came, left = refs[18], refs[19]
    fetches = [
        pltpu.make_async_copy(source, target, came.at[place])
        for place, (source, target) in enumerate(zip(sources, held))
    ]
    writes = [
        pltpu.make_async_copy(source, target, left.at[place])
        for place, (source, target) in enumerate(zip(held, targets))
    ]
    for fetch in fetches:
        fetch.start()
    for fetch, write in zip(fetches, writes):
        fetch.wait()
        write.start()
    for write in writes:
        write.wait()


def local(
    latents, cotangent, inner_edges, cut_cells, pair_count, in_weight, in_bias, out_weight, out_bias
):
    regions = lax.axis_size("region")
    subparts = lax.axis_size("sub")
    total = regions * subparts
    cell_count, channels = latents.shape
    edge_total = inner_edges.shape[1]
    wide, hidden = in_weight.shape
    narrow = out_weight.shape[0]
    lists = pair_count.shape[0]
    slots = cut_cells.shape[0] // lists
    cut_total = lists * slots
    block = 1024
    blocks = edge_total // block
    chunk = round_up(-(-(wide + narrow) // total), 8)
    slot_rows = round_up(chunk + 4, 16)
    vmem = pl.BlockSpec(memory_space=pltpu.VMEM)
    hbm = pl.BlockSpec(memory_space=pl.ANY)
    smem = pl.BlockSpec(memory_space=pltpu.SMEM)
    f32, bf16 = jnp.float32, jnp.bfloat16
    dma = pltpu.SemaphoreType.DMA
    results = pl.pallas_call(
        functools.partial(layer_kernel, regions, subparts, chunk, block),
        out_shape=[
            jax.ShapeDtypeStruct((cell_count, channels), bf16),
            jax.ShapeDtypeStruct((cell_count, channels), bf16),
            jax.ShapeDtypeStruct((wide, hidden), f32),
            jax.ShapeDtypeStruct((1, hidden), f32),
            jax.ShapeDtypeStruct((narrow, channels), f32),
            jax.ShapeDtypeStruct((1, channels), f32),
        ],
        in_specs=[hbm, hbm, hbm, vmem, smem, hbm, vmem, hbm, vmem],
        out_specs=[vmem] * 6,
        scratch_shapes=[
            pltpu.VMEM((cell_count, channels), bf16),
            pltpu.VMEM((cell_count, channels), bf16),
            pltpu.VMEM((2, edge_total), jnp.int32),
            pltpu.VMEM((1, cut_total), jnp.int32),
            pltpu.VMEM((wide, hidden), bf16),
            pltpu.VMEM((narrow, channels), bf16),
            dma((5,)),
            pltpu.VMEM((cell_count, 2 * channels), bf16),
            pltpu.VMEM((lists, slots, 2 * channels), bf16),
            pltpu.VMEM((lists, slots, 2 * channels), bf16),
            pltpu.VMEM((cut_total, 2 * channels), bf16),
            pltpu.VMEM((cut_total, 2 * channels), bf16),
            pltpu.VMEM((cut_total, channels), f32),
            pltpu.VMEM((cut_total, channels), f32),
            pltpu.VMEM((blocks, 2 * block, 2 * channels), bf16),
            pltpu.VMEM((cut_total, 2 * channels), bf16),
            pltpu.VMEM((cell_count, 2 * channels), f32),
            pltpu.VMEM((max(total * chunk, wide + narrow), channels), f32),
            pltpu.VMEM((hidden, wide), f32),
            pltpu.VMEM((8, channels), f32),
            pltpu.VMEM((total, slot_rows, channels), bf16),
            pltpu.VMEM((total, slot_rows, channels), bf16),
            pltpu.VMEM((total, slot_rows, channels), bf16),
            dma((lists,)),
            dma((lists,)),
            dma((total,)),
            dma((total,)),
            dma((total,)),
            dma((total,)),
        ],
        compiler_params=pltpu.CompilerParams(
            collective_id=0, has_side_effects=True, vmem_limit_bytes=60 * 1024 * 1024
        ),
    )(
        latents, cotangent, inner_edges, cut_cells, pair_count,
        in_weight, in_bias[None], out_weight, out_bias[None],
    )
    a, b, c, d, e, f = pl.pallas_call(
        hand_on,
        out_shape=[jax.ShapeDtypeStruct(result.shape, result.dtype) for result in results],
        in_specs=[hbm] * 6,
        out_specs=[hbm] * 6,
        scratch_shapes=[*(pltpu.VMEM(result.shape, result.dtype) for result in results), dma((6,)), dma((6,))],
        compiler_params=pltpu.CompilerParams(vmem_limit_bytes=60 * 1024 * 1024),
    )(*results)
    return a, b, c, d[0], e, f[0]


def solution(mesh):
    placed = (
        P(("groups", "region", "sub"), None),
        P(("groups", "region", "sub"), None),
        P(None, ("groups", "region", "sub")),
        P(("groups", "region", "sub")),
        P(("groups", "region", "sub")),
        P(),
        P(),
        P(),
        P(),
    )
    return jax.shard_map(
        local,
        mesh=mesh,
        in_specs=placed,
        out_specs=(
            P(("groups", "region", "sub"), None),
            P(("groups", "region", "sub"), None),
            P("groups", None),
            P("groups"),
            P("groups", None),
            P("groups"),
        ),
        check_vma=False,
    )
```
